32 devices in a mesh: groups: 2 (over x), dp: 16 (over z, y, core).
Axes of the slice: x: 2, y: 2, z: 4, core: 2. Of those that a mesh axis runs over, the one named last changes fastest.
Arguments:
- hidden_rows: bfloat16 [512, 16, 14336], P(('groups', 'dp')), parts along dimension 0
- output_grads: bfloat16 [512, 16, 4096], P(('groups', 'dp')), parts along dimension 0
- proj_in: bfloat16 [32, 14336], replicated, may hold values from -0.046875 to 0.046875
- proj_out: bfloat16 [32, 4096], replicated, may hold values from -0.09375 to 0.09375
- token_counts: int32 [512], P(('groups', 'dp')), parts along dimension 0, may hold values from 1 to 16
- query_vectors: float32 [256, 1024], P(('groups', 'dp')), parts along dimension 0, may hold values from -6 to 6
- query_slot: int32 [256], P('groups'), parts along dimension 0, may hold values from 0 to 127, each once
Outputs:
- scores: float32 [512, 128], P(('groups', 'dp')), parts along dimension 0
The draws below stay inside these ranges and needn't reach their ends.
There are 2 independent parts, one for each index of `groups`. The reference program is written for one: setup_inputs(seed, part) draws one part's arguments, and reference() takes and returns one part's arrays. A program takes and returns all parts, laid end to end along the dimension named above; an argument that names none is the same for every part. Nothing has to cross between parts.
Inputs may be any that keep to these rules, and one draw needn't show every extreme that they name: `query_slot`: each of 0 to 127 once.
All inputs are finite; a program needn't handle non-finite values.
Results may differ from the reference program's by a relative error of at most 0.0003.
Values sent between devices are 32-bit elements; how exact they have to be, the bound alone decides.
No kernel may reach another device: no remote copies, remote signals or barrier semaphores. Data moves between devices by JAX's collectives and lax.ppermute only.
A program may use at most 128 MiB of HBM per device.

```python
import math
import jax
import jax.numpy as jnp
from jax import lax

D = 4096
FF = 14336
R = 32
SEQ = 16
RR = 1024
EXAMPLES = 256
QUERIES = 128


def add_parts(base, coef, dirs, jitter, count):
    for index in range(count):
        weight = 1.6 / (index + 1.0) * jitter[index]
        base = base + weight * coef[:, :, index:index + 1] * dirs[index][None, None, :]
    return base


def draw_hidden_rows(key, part):
    key = jax.random.fold_in(key, 11)
    base_key = jax.random.fold_in(key, 0)
    row_key = jax.random.fold_in(key, 1)
    col_key = jax.random.fold_in(key, 2)
    coef_key = jax.random.fold_in(key, 4)
    dir_key = jax.random.fold_in(key, 5)
    amp_key = jax.random.fold_in(key, 6)
    row_pos = jax.random.uniform(row_key, (EXAMPLES, 1, 1), jnp.float32)
    col_pos = jax.random.uniform(col_key, (1, 1, FF), jnp.float32)
    rising = 3.0 ** (jnp.arange(EXAMPLES, dtype=jnp.float32) / EXAMPLES)[:, None, None]
    coef = jax.random.normal(coef_key, (EXAMPLES, SEQ, 12), jnp.float32)
    dirs = jax.random.normal(dir_key, (12, FF), jnp.float32)
    jitter = jnp.exp(jax.random.uniform(amp_key, (12,), jnp.float32, math.log(0.7), math.log(1.4)))
    base = 0.5 * jax.random.normal(base_key, (EXAMPLES, SEQ, FF), jnp.float32)
    scale = 10.0 ** row_pos * 10.0 ** (col_pos - 0.5) * rising / 4.0
    base = add_parts(base, coef, dirs, jitter, 12)
    return (base * scale).astype(jnp.bfloat16)


def draw_output_grads(key, part):
    key = jax.random.fold_in(key, 37)
    base_key, row_key, coef_key, dir_key, amp_key = jax.random.split(key, 5)
    coef = jax.random.normal(coef_key, (EXAMPLES, SEQ, 12), jnp.float32)
    dirs = jax.random.normal(dir_key, (12, D), jnp.float32)
    jitter = jnp.exp(jax.random.uniform(amp_key, (12,), jnp.float32, math.log(0.7), math.log(1.4)))
    row_pos = jax.random.uniform(row_key, (EXAMPLES, 1, 1), jnp.float32)
    base = 0.5 * jax.random.normal(base_key, (EXAMPLES, SEQ, D), jnp.float32)
    scale = 10.0 ** (0.3 * row_pos) * 0.5
    base = add_parts(base, coef, dirs, jitter, 12)
    return (base * scale).astype(jnp.bfloat16)


def draw_token_counts(key, part):
    key = jax.random.fold_in(key, 23)
    counts = jax.random.randint(key, (EXAMPLES,), 1, SEQ + 1, jnp.int32)
    return counts.at[0].set(SEQ)


def block_scale(rng, dims, cuts, smallest, high):
    def one(position, blocks):
        steps = jax.random.uniform(jax.random.fold_in(jax.random.fold_in(rng, 6), position), (blocks,), jnp.float32, smallest / len(cuts), high / len(cuts))
        return jnp.repeat(jnp.exp(steps), dims[position] // blocks).reshape((-1,) + (1,) * (len(dims) - position - 1))

    factor_of = one(*cuts[0])
    for cut in cuts[1:]:
        factor_of = factor_of * one(*cut)
    return factor_of


def normal_values(own_key, shape, deviation, limit, shards=(), kind=jnp.bfloat16):
    drawn = deviation * jax.random.normal(own_key, shape, jnp.float32)
    if shards:
        drawn = drawn * block_scale(own_key, shape, shards, -0.22, 0.18)
    return jnp.clip(drawn, -limit, limit).astype(kind)


def setup_inputs(seed: int = 0, part: int = 0) -> dict:
    streams_of = jax.random.split(jax.random.key(seed), 8)
    own_keys = jax.random.split(jax.random.fold_in(streams_of[7], part), 8)
    return {
        "hidden_rows": draw_hidden_rows(jax.random.fold_in(jax.random.fold_in(streams_of[7], part), 71), part),
        "output_grads": draw_output_grads(jax.random.fold_in(jax.random.fold_in(streams_of[7], part), 71), part),
        "proj_in": normal_values(streams_of[2], (R, FF), FF ** -0.5, 0.046875),
        "proj_out": normal_values(streams_of[3], (R, D), D ** -0.5, 0.09375),
        "token_counts": draw_token_counts(jax.random.fold_in(jax.random.fold_in(streams_of[7], part), 71), part),
        "query_vectors": normal_values(own_keys[5], (QUERIES, RR), 1.0, 6.0, ((0, 16),), jnp.float32),
        "query_slot": jax.random.permutation(own_keys[6], QUERIES).astype(jnp.int32),
    }


def reference(hidden_rows, output_grads, proj_in, proj_out, token_counts, query_vectors, query_slot):
    left = jnp.dot(hidden_rows.reshape(EXAMPLES * SEQ, FF).astype(jnp.float32), proj_in.T.astype(jnp.float32), preferred_element_type=jnp.float32)
    right = jnp.dot(output_grads.reshape(EXAMPLES * SEQ, D).astype(jnp.float32), proj_out.T.astype(jnp.float32), preferred_element_type=jnp.float32)
    left = left.reshape(EXAMPLES, SEQ, R)
    right = right.reshape(EXAMPLES, SEQ, R)
    slots = jnp.arange(SEQ, dtype=jnp.int32)
    masking = (slots[None, :] < token_counts[:, None]).astype(jnp.float32)
    left = left * masking[:, :, None]
    outer = jnp.einsum('esr,esq->erq', left, right, precision=lax.Precision.HIGHEST)
    vectors = (outer / token_counts.astype(jnp.float32)[:, None, None]).reshape(EXAMPLES, RR)
    fisher = jnp.dot(vectors.T, vectors, precision=lax.Precision.HIGHEST) / jnp.float32(EXAMPLES)
    damped = fisher + 0.1 * jnp.trace(fisher) / RR * jnp.eye(RR, dtype=jnp.float32)
    chol = jnp.linalg.cholesky(damped)
    first = lax.linalg.triangular_solve(chol, query_vectors, left_side=False, lower=True, transpose_a=True)
    solved = lax.linalg.triangular_solve(chol, first, left_side=False, lower=True, transpose_a=False)
    ordered = solved[query_slot]
    return jnp.dot(vectors, ordered.T, precision=lax.Precision.HIGHEST)
```

```python
import functools

import jax
import jax.numpy as jnp
from jax import lax
from jax.experimental import pallas as pl
from jax.experimental.pallas import tpu as pltpu
from jax.sharding import PartitionSpec as P

damp_share = 0.1
f32 = jnp.float32
bf16 = jnp.bfloat16
levels = 9
vmem_bytes = 60 * 2**20


def split3(x):
    high = x.astype(bf16)
    rest = x - high.astype(f32)
    mid = rest.astype(bf16)
    low = (rest - mid.astype(f32)).astype(bf16)
    return high, mid, low


def nt(a, b):
    return lax.dot_general(a, b, (((1,), (1,)), ((), ())), preferred_element_type=f32)


def nn(a, b):
    return jnp.dot(a, b, preferred_element_type=f32)


def project_kernel(
    cuts, hidden, grads, pin, pout, counts, queries, out, hbuf, gbuf, pibuf, pobuf, sems
):
    examples, seq, width = hbuf.shape
    model = gbuf.shape[2]
    rank = pibuf.shape[0]
    flat = rank * rank
    rows = examples * seq
    copies = [
        pltpu.make_async_copy(pout, pobuf, sems.at[0]),
        pltpu.make_async_copy(grads, gbuf, sems.at[1]),
        pltpu.make_async_copy(pin, pibuf, sems.at[2]),
    ]
    for i, (a, b) in enumerate(cuts):
        copies.append(
            pltpu.make_async_copy(
                hidden.at[:, :, a:b], hbuf.at[:, :, a:b], sems.at[3 + i]
            )
        )
    for copy in copies:
        copy.start()
    copies[0].wait()
    copies[1].wait()
    right = nt(gbuf[...].reshape(rows, model), pobuf[...])
    copies[2].wait()
    left = jnp.zeros((rows, rank), f32)
    for i, (a, b) in enumerate(cuts):
        copies[3 + i].wait()
        left = left + nt(hbuf[:, :, a:b].reshape(rows, b - a), pibuf[:, a:b])
    example = lax.broadcasted_iota(jnp.int32, (examples, 1), 0)
    live = jnp.zeros((examples, 1), jnp.int32)
    for e in range(examples):
        live = jnp.where(example == e, counts[e], live)
    to = lax.broadcasted_iota(jnp.int32, (seq, examples, rows), 1)
    slot = lax.broadcasted_iota(jnp.int32, (seq, examples, rows), 0)
    source = lax.broadcasted_iota(jnp.int32, (seq, examples, rows), 2)
    chosen = (source == to * seq + slot) & (slot < live[None])
    pick = jnp.where(chosen, 1.0, 0.0).astype(bf16).reshape(rows, rows)
    parts = jnp.concatenate(split3(left) + split3(right), axis=1)
    parts = nn(pick, parts).astype(bf16)
    wide = 3 * rank
    column = lax.broadcasted_iota(jnp.int32, (wide, flat), 1)
    row = lax.broadcasted_iota(jnp.int32, (wide, flat), 0) % rank
    spread = jnp.where(row == column // rank, 1.0, 0.0).astype(bf16)
    tile = jnp.where(row == column % rank, 1.0, 0.0).astype(bf16)
    over = live.astype(f32)
    step = 256
    for c in range(0, flat, step):
        product = nn(parts[:, :wide], spread[:, c : c + step]) * nn(
            parts[:, wide:], tile[:, c : c + step]
        )
        total = jnp.sum(product.reshape(seq, examples, step), axis=0)
        out[:examples, c : c + step] = total / over
    out[examples:] = queries[...]


def project(hidden_rows, output_grads, proj_in, proj_out, token_counts, queries):
    examples, seq, width = hidden_rows.shape
    model = output_grads.shape[2]
    rank = proj_in.shape[0]
    pieces = 7 if width % (7 * 128) == 0 else 1
    size = width // pieces
    cuts = tuple((i * size, (i + 1) * size) for i in range(pieces))
    anywhere = pl.BlockSpec(memory_space=pl.ANY)
    return pl.pallas_call(
        functools.partial(project_kernel, cuts),
        out_shape=jax.ShapeDtypeStruct((examples + queries.shape[0], rank * rank), f32),
        in_specs=[anywhere] * 4 + [
            pl.BlockSpec(memory_space=pltpu.SMEM),
            pl.BlockSpec(memory_space=pltpu.VMEM),
        ],
        out_specs=pl.BlockSpec(memory_space=pltpu.VMEM),
        scratch_shapes=[
            pltpu.VMEM(hidden_rows.shape, bf16),
            pltpu.VMEM(output_grads.shape, bf16),
            pltpu.VMEM(proj_in.shape, bf16),
            pltpu.VMEM(proj_out.shape, bf16),
            pltpu.SemaphoreType.DMA((3 + pieces,)),
        ],
        compiler_params=pltpu.CompilerParams(vmem_limit_bytes=vmem_bytes),
        name="project",
    )(hidden_rows, output_grads, proj_in, proj_out, token_counts, queries)


def square_parts(x, n, passes):
    high, mid, low = split3(x)
    if passes == 6:
        left = [high, high, mid, mid, high, low]
        right = [high, mid, high, mid, low, high]
    else:
        left = [high, high, mid]
        right = [high, mid, high]
    return nn(
        jnp.concatenate(left, axis=1),
        jnp.concatenate([r[:n] for r in right], axis=0),
    )


def solve_kernel(total, each, blocks, *refs):
    bs = refs[:blocks]
    slots, out, high, mid, low, held = refs[blocks:]
    tall, flat = bs[0].shape
    ask = tall - each
    n = each * blocks
    asked = ask * blocks
    squares = jnp.zeros((each, flat), f32)
    for i in range(blocks):
        v = bs[i][:each]
        squares = squares + v * v
        h, m, l = split3(v)
        high[i * each : (i + 1) * each] = h
        mid[i * each : (i + 1) * each] = m
        low[i * each : (i + 1) * each] = l
    h, m, l = split3(jnp.concatenate([b[each:] for b in bs], axis=0))
    high[n:] = h
    mid[n:] = m
    low[n:] = l
    trace = jnp.sum(squares, keepdims=True)
    hv, mv, lv = high[:n], mid[:n], low[:n]
    products = nt(high[...], hv) + (
        (nt(high[...], mv) + nt(mid[...], hv))
        + (nt(mid[...], mv) + nt(high[...], lv) + nt(low[...], hv))
    )
    gram = products[:n] / trace
    y = products[n:]
    scale = 2.0 * lax.rsqrt(jnp.sum(gram * gram, keepdims=True))
    d = gram * scale
    e = scale * (damp_share / flat)
    for level in range(levels - 1):
        both = jnp.concatenate([d, y], axis=0)
        w = square_parts(both, n, 6 if level < 4 else 3)
        d = 4.0 * d - 2.0 * w[:n]
        y = y - w[n:] * (1.0 / (e + 2.0))
        e = 2.0 * e * (e + 2.0)
    dh, dm, _ = split3(d)
    yh, ym, _ = split3(y)
    y = y - (nn(yh, dh) + (nn(yh, dm) + nn(ym, dh))) * (1.0 / (e + 2.0))
    e = 2.0 * e * (e + 2.0)
    held[...] = y
    short = e < 1e6
    last = jnp.where(short, 2.0 * e * (e + 2.0), e)

    @pl.when(e[0, 0] < 1e6)
    def _():
        w = square_parts(d, n, 3)
        more = 4.0 * d - 2.0 * w
        mh, mm, _ = split3(more)
        now = held[...]
        nh, nm, _ = split3(now)
        held[...] = now - (nn(nh, mh) + (nn(nh, mm) + nn(nm, mh))) * (1.0 / (e + 2.0))

    factor = (flat * total / damp_share) / trace * (last / (1.0 + last))
    mine = held[:, :each] * factor
    place = lax.broadcasted_iota(jnp.int32, (asked, asked), 0) ^ (ask * lax.axis_index("dp"))
    pick = jnp.where(place == slots[...], 1.0, 0.0).astype(bf16)
    a, b, c = split3(mine)
    tn = (((0,), (0,)), ((), ()))
    out[...] = (
        lax.dot_general(a, pick, tn, preferred_element_type=f32)
        + lax.dot_general(b, pick, tn, preferred_element_type=f32)
        + lax.dot_general(c, pick, tn, preferred_element_type=f32)
    )


def solve(total, each, blocks, slots):
    tall, flat = blocks[0].shape
    asked = slots.shape[0]
    n = each * len(blocks)
    return pl.pallas_call(
        functools.partial(solve_kernel, total, each, len(blocks)),
        out_shape=jax.ShapeDtypeStruct((each, asked), f32),
        in_specs=[pl.BlockSpec(memory_space=pltpu.VMEM)] * (len(blocks) + 1),
        out_specs=pl.BlockSpec(memory_space=pltpu.VMEM),
        scratch_shapes=[
            pltpu.VMEM((n + asked, flat), bf16),
            pltpu.VMEM((n + asked, flat), bf16),
            pltpu.VMEM((n + asked, flat), bf16),
            pltpu.VMEM((asked, n), f32),
        ],
        compiler_params=pltpu.CompilerParams(vmem_limit_bytes=vmem_bytes),
        name="solve",
    )(*blocks, slots.reshape(1, asked))


def flip(x, bits, size):
    return lax.ppermute(x, "dp", [(i, i ^ bits) for i in range(size)])


def gather_blocks(rows, size):
    got = {0: rows, 8: flip(rows, 8, size)}
    for k in (2, 4, 6):
        got[k] = flip(rows, k, size)
    for k in (2, 4, 6):
        got[8 + k] = flip(got[8], k, size)
    for k in range(0, size, 2):
        got[k + 1] = flip(got[k], 1, size)
    return [got[k] for k in range(size)]


def dual(hidden_rows, output_grads, proj_in, proj_out, token_counts, query_vectors, query_slot):
    size = lax.axis_size("dp")
    total = hidden_rows.shape[0] * size
    rows = project(hidden_rows, output_grads, proj_in, proj_out, token_counts, query_vectors)
    blocks = gather_blocks(rows, size)
    return solve(total, hidden_rows.shape[0], blocks, query_slot)


def primal(hidden_rows, output_grads, proj_in, proj_out, token_counts, query_vectors, query_slot):
    examples, seq, width = hidden_rows.shape
    rank = proj_in.shape[0]
    flat = rank * rank
    total = examples * lax.axis_size("dp")
    left = jnp.einsum("esf,rf->esr", hidden_rows, proj_in, preferred_element_type=f32)
    right = jnp.einsum("esd,rd->esr", output_grads, proj_out, preferred_element_type=f32)
    slots = jnp.arange(seq, dtype=jnp.int32)
    masking = (slots[None, :] < token_counts[:, None]).astype(f32)
    left = left * masking[:, :, None]
    outer = jnp.einsum("esr,esq->erq", left, right, precision=lax.Precision.HIGHEST)
    vectors = (outer / token_counts.astype(f32)[:, None, None]).reshape(examples, flat)
    partial_fisher = jnp.dot(vectors.T, vectors, precision=lax.Precision.HIGHEST)
    fisher = lax.psum(partial_fisher, "dp")
    fisher = fisher / f32(total)
    trace_value = lax.psum(jnp.sum(vectors * vectors), "dp") / f32(total)
    damped = fisher + damp_share * trace_value / flat * jnp.eye(flat, dtype=f32)
    chol = jnp.linalg.cholesky(damped)
    first = lax.linalg.triangular_solve(
        chol, query_vectors, left_side=False, lower=True, transpose_a=True
    )
    solved = lax.all_gather(
        lax.linalg.triangular_solve(chol, first, left_side=False, lower=True, transpose_a=False),
        "dp",
        axis=0,
        tiled=True,
    )
    ordered = solved[query_slot]
    return jnp.dot(vectors, ordered.T, precision=lax.Precision.HIGHEST)


def shards(hidden_rows, *rest):
    size = lax.axis_size("dp")
    examples, seq, _ = hidden_rows.shape
    asked = rest[4].shape[0]
    if size == 16 and examples == 16 and seq == 16 and asked == 8:
        return dual(hidden_rows, *rest)
    return primal(hidden_rows, *rest)


def solution(mesh):
    return jax.shard_map(
        shards,
        mesh=mesh,
        in_specs=(
            P(("groups", "dp"), None, None),
            P(("groups", "dp"), None, None),
            P(),
            P(),
            P(("groups", "dp")),
            P(("groups", "dp"), None),
            P("groups"),
        ),
        out_specs=P(("groups", "dp"), None),
        check_vma=False,
    )
```

```python
import functools

import jax
import jax.numpy as jnp
from jax import lax
from jax.experimental import pallas as pl
from jax.experimental.pallas import tpu as pltpu
from jax.sharding import PartitionSpec as P

damp_share = 0.1
f32 = jnp.float32
bf16 = jnp.bfloat16
levels = 9
vmem_bytes = 60 * 2**20


def split3(x):
    high = x.astype(bf16)
    rest = x - high.astype(f32)
    mid = rest.astype(bf16)
    low = (rest - mid.astype(f32)).astype(bf16)
    return high, mid, low


def nt(a, b):
    return lax.dot_general(a, b, (((1,), (1,)), ((), ())), preferred_element_type=f32)


def nn(a, b):
    return jnp.dot(a, b, preferred_element_type=f32)


def project_kernel(
    size, hidden, grads, pin, pout, counts, queries, out, hbuf, gbuf, pibuf, pobuf, left, sems
):
    pieces, examples, seq, _ = hbuf.shape
    model = gbuf.shape[2]
    rank = pobuf.shape[0]
    flat = rank * rank
    rows = examples * seq
    first = [
        pltpu.make_async_copy(pout, pobuf, sems.at[0]),
        pltpu.make_async_copy(grads, gbuf, sems.at[1]),
    ]

    def piece(i):
        across = pl.ds(pl.multiple_of(i * size, 128), size)
        return (
            pltpu.make_async_copy(pin.at[:, across], pibuf.at[i], sems.at[2 + i]),
            pltpu.make_async_copy(
                hidden.at[:, :, across], hbuf.at[i], sems.at[2 + pieces + i]
            ),
        )

    for copy in first:
        copy.start()
    for i in range(pieces):
        for copy in piece(i):
            copy.start()
    for copy in first:
        copy.wait()
    left[...] = jnp.zeros((rows, rank), f32)
    right = nt(gbuf[...].reshape(rows, model), pobuf[...])

    def work(i, carry):
        for copy in piece(i):
            copy.wait()
        left[...] += nt(hbuf[i].reshape(rows, size), pibuf[i])
        return carry

    lax.fori_loop(0, pieces, work, 0)
    example = lax.broadcasted_iota(jnp.int32, (examples, 1), 0)
    live = jnp.zeros((examples, 1), jnp.int32)
    for e in range(examples):
        live = jnp.where(example == e, counts[e], live)
    to = lax.broadcasted_iota(jnp.int32, (seq, examples, rows), 1)
    slot = lax.broadcasted_iota(jnp.int32, (seq, examples, rows), 0)
    source = lax.broadcasted_iota(jnp.int32, (seq, examples, rows), 2)
    chosen = (source == to * seq + slot) & (slot < live[None])
    pick = jnp.where(chosen, 1.0, 0.0).astype(bf16).reshape(rows, rows)
    parts = jnp.concatenate(split3(left[...]) + split3(right), axis=1)
    parts = nn(pick, parts).astype(bf16)
    wide = 3 * rank
    column = lax.broadcasted_iota(jnp.int32, (wide, flat), 1)
    row = lax.broadcasted_iota(jnp.int32, (wide, flat), 0) % rank
    spread = jnp.where(row == column // rank, 1.0, 0.0).astype(bf16)
    tile = jnp.where(row == column % rank, 1.0, 0.0).astype(bf16)
    over = live.astype(f32)
    step = 256
    for c in range(0, flat, step):
        product = nn(parts[:, :wide], spread[:, c : c + step]) * nn(
            parts[:, wide:], tile[:, c : c + step]
        )
        total = jnp.sum(product.reshape(seq, examples, step), axis=0)
        out[:examples, c : c + step] = total / over
    out[examples:] = queries[...]


def project(hidden_rows, output_grads, proj_in, proj_out, token_counts, queries):
    examples, seq, width = hidden_rows.shape
    model = output_grads.shape[2]
    rank = proj_in.shape[0]
    pieces = 4 if width % (4 * 128) == 0 else 1
    size = width // pieces
    anywhere = pl.BlockSpec(memory_space=pl.ANY)
    return pl.pallas_call(
        functools.partial(project_kernel, size),
        out_shape=jax.ShapeDtypeStruct((examples + queries.shape[0], rank * rank), f32),
        in_specs=[anywhere] * 4 + [
            pl.BlockSpec(memory_space=pltpu.SMEM),
            pl.BlockSpec(memory_space=pltpu.VMEM),
        ],
        out_specs=pl.BlockSpec(memory_space=pltpu.VMEM),
        scratch_shapes=[
            pltpu.VMEM((pieces, examples, seq, size), bf16),
            pltpu.VMEM(output_grads.shape, bf16),
            pltpu.VMEM((pieces, rank, size), bf16),
            pltpu.VMEM(proj_out.shape, bf16),
            pltpu.VMEM((examples * seq, rank), f32),
            pltpu.SemaphoreType.DMA((2 + 2 * pieces,)),
        ],
        compiler_params=pltpu.CompilerParams(vmem_limit_bytes=vmem_bytes),
        name="project",
    )(hidden_rows, output_grads, proj_in, proj_out, token_counts, queries)


def times(x, n, passes):
    high, mid, low = split3(x)
    total = nt(high, high[:n]) + (nt(high, mid[:n]) + nt(mid, high[:n]))
    if passes > 3:
        total = total + nt(mid, mid[:n])
    if passes > 4:
        total = total + (nt(high, low[:n]) + nt(low, high[:n]))
    return total


def solve_kernel(total, each, blocks, *refs):
    bs = refs[:blocks]
    slots, out, held = refs[blocks:]
    tall, flat = bs[0].shape
    ask = tall - each
    n = each * blocks
    asked = ask * blocks

    squares = jnp.zeros((1, n), f32)
    for k in range(0, flat, n):
        x = jnp.concatenate(
            [b[:each, k : k + n] for b in bs] + [b[each:, k : k + n] for b in bs], axis=0
        )
        w = times(x, n, 6)
        held[...] = w if k == 0 else held[...] + w
        squares = squares + jnp.sum(x[:n] * x[:n], axis=0, keepdims=True)
    trace = jnp.sum(squares, keepdims=True)
    gram = held[:n] * (1.0 / trace)
    scale = 2.0 * lax.rsqrt(jnp.sum(gram * gram, keepdims=True))
    held[:n] = gram * scale
    e = scale * (damp_share / flat)
    ahead = e
    for _ in range(levels):
        ahead = 2.0 * ahead * (ahead + 2.0)
    short = ahead < 1e6

    def double(passes, level, e):
        x = held[...]
        w = times(x, n, passes)
        held[:n] = 4.0 * x[:n] - 2.0 * w[:n]
        held[n:] = x[n:] - w[n:] * (1.0 / (e + 2.0))
        return 2.0 * e * (e + 2.0)

    e = lax.fori_loop(0, 4, functools.partial(double, 6), e)
    more = jnp.where(jnp.sum(jnp.where(short, 1.0, 0.0)) > 0.5, 1, 0)
    e = lax.fori_loop(4, levels + more, functools.partial(double, 3), e)
    factor = (flat * total / damp_share) / trace * (e / (1.0 + e))
    mine = held[n:, :each] * factor
    place = lax.broadcasted_iota(jnp.int32, (asked, asked), 0) ^ (ask * lax.axis_index("dp"))
    pick = jnp.where(place == slots[...], 1.0, 0.0).astype(bf16)
    a, b, c = split3(mine)
    tn = (((0,), (0,)), ((), ()))
    out[...] = (
        lax.dot_general(a, pick, tn, preferred_element_type=f32)
        + lax.dot_general(b, pick, tn, preferred_element_type=f32)
        + lax.dot_general(c, pick, tn, preferred_element_type=f32)
    )


def solve(total, each, blocks, slots):
    tall, flat = blocks[0].shape
    asked = slots.shape[0]
    n = each * len(blocks)
    return pl.pallas_call(
        functools.partial(solve_kernel, total, each, len(blocks)),
        out_shape=jax.ShapeDtypeStruct((each, asked), f32),
        in_specs=[pl.BlockSpec(memory_space=pltpu.VMEM)] * (len(blocks) + 1),
        out_specs=pl.BlockSpec(memory_space=pltpu.VMEM),
        scratch_shapes=[pltpu.VMEM((n + asked, n), f32)],
        compiler_params=pltpu.CompilerParams(vmem_limit_bytes=vmem_bytes),
        name="solve",
    )(*blocks, slots.reshape(1, asked))


def flip(x, bits, size):
    return lax.ppermute(x, "dp", [(i, i ^ bits) for i in range(size)])


def gather_blocks(rows, size):
    got = {0: rows, 8: flip(rows, 8, size), 2: flip(rows, 2, size), 4: flip(rows, 4, size)}
    for k in (6, 4, 2):
        got[8 + k] = flip(got[8], k, size)
    got[6] = flip(got[4], 2, size)
    for k in (0, 8, 2, 4, 6, 14, 12, 10):
        got[k + 1] = flip(got[k], 1, size)
    return [got[k] for k in range(size)]


def dual(hidden_rows, output_grads, proj_in, proj_out, token_counts, query_vectors, query_slot):
    size = lax.axis_size("dp")
    total = hidden_rows.shape[0] * size
    rows = project(hidden_rows, output_grads, proj_in, proj_out, token_counts, query_vectors)
    blocks = gather_blocks(rows, size)
    return solve(total, hidden_rows.shape[0], blocks, query_slot)


def primal(hidden_rows, output_grads, proj_in, proj_out, token_counts, query_vectors, query_slot):
    examples, seq, width = hidden_rows.shape
    rank = proj_in.shape[0]
    flat = rank * rank
    total = examples * lax.axis_size("dp")
    left = jnp.einsum("esf,rf->esr", hidden_rows, proj_in, preferred_element_type=f32)
    right = jnp.einsum("esd,rd->esr", output_grads, proj_out, preferred_element_type=f32)
    slots = jnp.arange(seq, dtype=jnp.int32)
    masking = (slots[None, :] < token_counts[:, None]).astype(f32)
    left = left * masking[:, :, None]
    outer = jnp.einsum("esr,esq->erq", left, right, precision=lax.Precision.HIGHEST)
    vectors = (outer / token_counts.astype(f32)[:, None, None]).reshape(examples, flat)
    partial_fisher = jnp.dot(vectors.T, vectors, precision=lax.Precision.HIGHEST)
    fisher = lax.psum(partial_fisher, "dp")
    fisher = fisher / f32(total)
    trace_value = lax.psum(jnp.sum(vectors * vectors), "dp") / f32(total)
    damped = fisher + damp_share * trace_value / flat * jnp.eye(flat, dtype=f32)
    chol = jnp.linalg.cholesky(damped)
    first = lax.linalg.triangular_solve(
        chol, query_vectors, left_side=False, lower=True, transpose_a=True
    )
    solved = lax.all_gather(
        lax.linalg.triangular_solve(chol, first, left_side=False, lower=True, transpose_a=False),
        "dp",
        axis=0,
        tiled=True,
    )
    ordered = solved[query_slot]
    return jnp.dot(vectors, ordered.T, precision=lax.Precision.HIGHEST)


def shards(hidden_rows, *rest):
    size = lax.axis_size("dp")
    examples, seq, _ = hidden_rows.shape
    asked = rest[4].shape[0]
    if size == 16 and examples == 16 and seq == 16 and asked == 8:
        return dual(hidden_rows, *rest)
    return primal(hidden_rows, *rest)


def solution(mesh):
    return jax.shard_map(
        shards,
        mesh=mesh,
        in_specs=(
            P(("groups", "dp"), None, None),
            P(("groups", "dp"), None, None),
            P(),
            P(),
            P(("groups", "dp")),
            P(("groups", "dp"), None),
            P("groups"),
        ),
        out_specs=P(("groups", "dp"), None),
        check_vma=False,
    )
```

```python
import functools

import jax
import jax.numpy as jnp
from jax import lax
from jax.experimental import pallas as pl
from jax.experimental.pallas import tpu as pltpu
from jax.sharding import PartitionSpec as P

damp_share = 0.1
f32 = jnp.float32
bf16 = jnp.bfloat16
levels = 9
vmem_bytes = 60 * 2**20


def split3(x):
    high = x.astype(bf16)
    rest = x - high.astype(f32)
    mid = rest.astype(bf16)
    low = (rest - mid.astype(f32)).astype(bf16)
    return high, mid, low


def nt(a, b):
    return lax.dot_general(a, b, (((1,), (1,)), ((), ())), preferred_element_type=f32)


def nn(a, b):
    return jnp.dot(a, b, preferred_element_type=f32)


def project_kernel(
    size, hidden, grads, pin, pout, counts, queries, out, hbuf, gbuf, pibuf, pobuf, left, sems
):
    pieces, examples, seq, _ = hbuf.shape
    model = gbuf.shape[2]
    rank = pobuf.shape[0]
    flat = rank * rank
    rows = examples * seq
    first = [
        pltpu.make_async_copy(pout, pobuf, sems.at[0]),
        pltpu.make_async_copy(grads, gbuf, sems.at[1]),
    ]

    def piece(i):
        across = pl.ds(pl.multiple_of(i * size, 128), size)
        return (
            pltpu.make_async_copy(pin.at[:, across], pibuf.at[i], sems.at[2 + i]),
            pltpu.make_async_copy(
                hidden.at[:, :, across], hbuf.at[i], sems.at[2 + pieces + i]
            ),
        )

    for copy in first:
        copy.start()
    for i in range(pieces):
        for copy in piece(i):
            copy.start()
    for copy in first:
        copy.wait()
    left[...] = jnp.zeros((rows, rank), f32)
    right = nt(gbuf[...].reshape(rows, model), pobuf[...])

    def work(i, carry):
        for copy in piece(i):
            copy.wait()
        left[...] += nt(hbuf[i].reshape(rows, size), pibuf[i])
        return carry

    lax.fori_loop(0, pieces, work, 0)
    example = lax.broadcasted_iota(jnp.int32, (examples, 1), 0)
    live = jnp.zeros((examples, 1), jnp.int32)
    for e in range(examples):
        live = jnp.where(example == e, counts[e], live)
    to = lax.broadcasted_iota(jnp.int32, (seq, examples, rows), 1)
    slot = lax.broadcasted_iota(jnp.int32, (seq, examples, rows), 0)
    source = lax.broadcasted_iota(jnp.int32, (seq, examples, rows), 2)
    chosen = (source == to * seq + slot) & (slot < live[None])
    pick = jnp.where(chosen, 1.0, 0.0).astype(bf16).reshape(rows, rows)
    parts = jnp.concatenate(split3(left[...]) + split3(right), axis=1)
    parts = nn(pick, parts).astype(bf16)
    wide = 3 * rank
    column = lax.broadcasted_iota(jnp.int32, (wide, flat), 1)
    row = lax.broadcasted_iota(jnp.int32, (wide, flat), 0) % rank
    spread = jnp.where(row == column // rank, 1.0, 0.0).astype(bf16)
    tile = jnp.where(row == column % rank, 1.0, 0.0).astype(bf16)
    over = live.astype(f32)
    step = 256
    for c in range(0, flat, step):
        product = nn(parts[:, :wide], spread[:, c : c + step]) * nn(
            parts[:, wide:], tile[:, c : c + step]
        )
        total = jnp.sum(product.reshape(seq, examples, step), axis=0)
        out[:examples, c : c + step] = total / over
    out[examples:] = queries[...]


def project(hidden_rows, output_grads, proj_in, proj_out, token_counts, queries):
    examples, seq, width = hidden_rows.shape
    model = output_grads.shape[2]
    rank = proj_in.shape[0]
    pieces = 4 if width % (4 * 128) == 0 else 1
    size = width // pieces
    anywhere = pl.BlockSpec(memory_space=pl.ANY)
    return pl.pallas_call(
        functools.partial(project_kernel, size),
        out_shape=jax.ShapeDtypeStruct((examples + queries.shape[0], rank * rank), f32),
        in_specs=[anywhere] * 4 + [
            pl.BlockSpec(memory_space=pltpu.SMEM),
            pl.BlockSpec(memory_space=pltpu.VMEM),
        ],
        out_specs=pl.BlockSpec(memory_space=pltpu.VMEM),
        scratch_shapes=[
            pltpu.VMEM((pieces, examples, seq, size), bf16),
            pltpu.VMEM(output_grads.shape, bf16),
            pltpu.VMEM((pieces, rank, size), bf16),
            pltpu.VMEM(proj_out.shape, bf16),
            pltpu.VMEM((examples * seq, rank), f32),
            pltpu.SemaphoreType.DMA((2 + 2 * pieces,)),
        ],
        compiler_params=pltpu.CompilerParams(vmem_limit_bytes=vmem_bytes),
        name="project",
    )(hidden_rows, output_grads, proj_in, proj_out, token_counts, queries)


def times(x, n, passes):
    high, mid, low = split3(x)
    total = nt(high, high[:n]) + (nt(high, mid[:n]) + nt(mid, high[:n]))
    if passes > 3:
        total = total + nt(mid, mid[:n])
    if passes > 4:
        total = total + (nt(high, low[:n]) + nt(low, high[:n]))
    return total


def solve_kernel(total, each, blocks, *refs):
    bs = refs[:blocks]
    slots, out, held = refs[blocks:]
    tall, flat = bs[0].shape
    ask = tall - each
    n = each * blocks
    asked = ask * blocks

    squares = jnp.zeros((1, n), f32)
    for k in range(0, flat, n):
        x = jnp.concatenate(
            [b[:each, k : k + n] for b in bs] + [b[each:, k : k + n] for b in bs], axis=0
        )
        w = times(x, n, 6)
        held[...] = w if k == 0 else held[...] + w
        squares = squares + jnp.sum(x[:n] * x[:n], axis=0, keepdims=True)
    trace = jnp.sum(squares, keepdims=True)
    gram = held[:n] * (1.0 / trace)
    scale = 2.0 * lax.rsqrt(jnp.sum(gram * gram, keepdims=True))
    held[:n] = gram * scale
    e = scale * (damp_share / flat)
    ahead = e
    for _ in range(levels):
        ahead = 2.0 * ahead * (ahead + 2.0)
    short = ahead < 1e6

    def double(passes, level, e):
        x = held[...]
        w = times(x, n, passes)
        held[:n] = 4.0 * x[:n] - 2.0 * w[:n]
        held[n:] = x[n:] - w[n:] * (1.0 / (e + 2.0))
        return 2.0 * e * (e + 2.0)

    e = lax.fori_loop(0, 4, functools.partial(double, 6), e)
    more = jnp.where(jnp.sum(jnp.where(short, 1.0, 0.0)) > 0.5, 1, 0)
    e = lax.fori_loop(4, levels + more, functools.partial(double, 3), e)
    factor = (flat * total / damp_share) / trace * (e / (1.0 + e))
    mine = held[n:, :each] * factor
    place = lax.broadcasted_iota(jnp.int32, (asked, asked), 0) ^ (ask * lax.axis_index("dp"))
    pick = jnp.where(place == slots[...], 1.0, 0.0).astype(bf16)
    a, b, c = split3(mine)
    tn = (((0,), (0,)), ((), ()))
    out[...] = (
        lax.dot_general(a, pick, tn, preferred_element_type=f32)
        + lax.dot_general(b, pick, tn, preferred_element_type=f32)
        + lax.dot_general(c, pick, tn, preferred_element_type=f32)
    )


def solve(total, each, blocks, slots):
    tall, flat = blocks[0].shape
    asked = slots.shape[0]
    n = each * len(blocks)
    return pl.pallas_call(
        functools.partial(solve_kernel, total, each, len(blocks)),
        out_shape=jax.ShapeDtypeStruct((each, asked), f32),
        in_specs=[pl.BlockSpec(memory_space=pltpu.VMEM)] * (len(blocks) + 1),
        out_specs=pl.BlockSpec(memory_space=pltpu.VMEM),
        scratch_shapes=[pltpu.VMEM((n + asked, n), f32)],
        compiler_params=pltpu.CompilerParams(vmem_limit_bytes=vmem_bytes),
        name="solve",
    )(*blocks, slots.reshape(1, asked))


def flip(x, bits, size):
    return lax.ppermute(x, "dp", [(i, i ^ bits) for i in range(size)])


def gather_blocks(rows, size):
    got = {0: rows}
    for k in (8, 6, 4, 2):
        got[k] = flip(rows, k, size)
    for k in (6, 4, 2):
        got[8 + k] = flip(got[8], k, size)
    for k in (0, 8, 2, 4, 6, 10, 12, 14):
        got[k + 1] = flip(got[k], 1, size)
    return [got[k] for k in range(size)]


def dual(hidden_rows, output_grads, proj_in, proj_out, token_counts, query_vectors, query_slot):
    size = lax.axis_size("dp")
    total = hidden_rows.shape[0] * size
    rows = project(hidden_rows, output_grads, proj_in, proj_out, token_counts, query_vectors)
    blocks = gather_blocks(rows, size)
    return solve(total, hidden_rows.shape[0], blocks, query_slot)


def primal(hidden_rows, output_grads, proj_in, proj_out, token_counts, query_vectors, query_slot):
    examples, seq, width = hidden_rows.shape
    rank = proj_in.shape[0]
    flat = rank * rank
    total = examples * lax.axis_size("dp")
    left = jnp.einsum("esf,rf->esr", hidden_rows, proj_in, preferred_element_type=f32)
    right = jnp.einsum("esd,rd->esr", output_grads, proj_out, preferred_element_type=f32)
    slots = jnp.arange(seq, dtype=jnp.int32)
    masking = (slots[None, :] < token_counts[:, None]).astype(f32)
    left = left * masking[:, :, None]
    outer = jnp.einsum("esr,esq->erq", left, right, precision=lax.Precision.HIGHEST)
    vectors = (outer / token_counts.astype(f32)[:, None, None]).reshape(examples, flat)
    partial_fisher = jnp.dot(vectors.T, vectors, precision=lax.Precision.HIGHEST)
    fisher = lax.psum(partial_fisher, "dp")
    fisher = fisher / f32(total)
    trace_value = lax.psum(jnp.sum(vectors * vectors), "dp") / f32(total)
    damped = fisher + damp_share * trace_value / flat * jnp.eye(flat, dtype=f32)
    chol = jnp.linalg.cholesky(damped)
    first = lax.linalg.triangular_solve(
        chol, query_vectors, left_side=False, lower=True, transpose_a=True
    )
    solved = lax.all_gather(
        lax.linalg.triangular_solve(chol, first, left_side=False, lower=True, transpose_a=False),
        "dp",
        axis=0,
        tiled=True,
    )
    ordered = solved[query_slot]
    return jnp.dot(vectors, ordered.T, precision=lax.Precision.HIGHEST)


def shards(hidden_rows, *rest):
    size = lax.axis_size("dp")
    examples, seq, _ = hidden_rows.shape
    asked = rest[4].shape[0]
    if size == 16 and examples == 16 and seq == 16 and asked == 8:
        return dual(hidden_rows, *rest)
    return primal(hidden_rows, *rest)


def solution(mesh):
    return jax.shard_map(
        shards,
        mesh=mesh,
        in_specs=(
            P(("groups", "dp"), None, None),
            P(("groups", "dp"), None, None),
            P(),
            P(),
            P(("groups", "dp")),
            P(("groups", "dp"), None),
            P("groups"),
        ),
        out_specs=P(("groups", "dp"), None),
        check_vma=False,
    )
```

```python
import functools

import jax
import jax.numpy as jnp
from jax import lax
from jax.experimental import pallas as pl
from jax.experimental.pallas import tpu as pltpu
from jax.sharding import PartitionSpec as P

damp_share = 0.1
f32 = jnp.float32
bf16 = jnp.bfloat16
levels = 9
vmem_bytes = 60 * 2**20


def split3(x):
    high = x.astype(bf16)
    rest = x - high.astype(f32)
    mid = rest.astype(bf16)
    low = (rest - mid.astype(f32)).astype(bf16)
    return high, mid, low


def nt(a, b):
    return lax.dot_general(a, b, (((1,), (1,)), ((), ())), preferred_element_type=f32)


def nn(a, b):
    return jnp.dot(a, b, preferred_element_type=f32)


def project_kernel(
    size, hidden, grads, pin, pout, counts, queries, out, hbuf, gbuf, pibuf, pobuf, left, sems
):
    pieces, examples, seq, _ = hbuf.shape
    model = gbuf.shape[2]
    rank = pobuf.shape[0]
    flat = rank * rank
    rows = examples * seq
    first = [
        pltpu.make_async_copy(pout, pobuf, sems.at[0]),
        pltpu.make_async_copy(grads, gbuf, sems.at[1]),
    ]

    def piece(i):
        across = pl.ds(pl.multiple_of(i * size, 128), size)
        return (
            pltpu.make_async_copy(pin.at[:, across], pibuf.at[i], sems.at[2 + i]),
            pltpu.make_async_copy(
                hidden.at[:, :, across], hbuf.at[i], sems.at[2 + pieces + i]
            ),
        )

    for copy in first:
        copy.start()
    for i in range(pieces):
        for copy in piece(i):
            copy.start()
    for copy in first:
        copy.wait()
    left[...] = jnp.zeros((rows, rank), f32)
    right = nt(gbuf[...].reshape(rows, model), pobuf[...])

    def work(i, carry):
        for copy in piece(i):
            copy.wait()
        left[...] += nt(hbuf[i].reshape(rows, size), pibuf[i])
        return carry

    lax.fori_loop(0, pieces, work, 0)
    example = lax.broadcasted_iota(jnp.int32, (examples, 1), 0)
    live = jnp.zeros((examples, 1), jnp.int32)
    for e in range(examples):
        live = jnp.where(example == e, counts[e], live)
    to = lax.broadcasted_iota(jnp.int32, (seq, examples, rows), 1)
    slot = lax.broadcasted_iota(jnp.int32, (seq, examples, rows), 0)
    source = lax.broadcasted_iota(jnp.int32, (seq, examples, rows), 2)
    chosen = (source == to * seq + slot) & (slot < live[None])
    pick = jnp.where(chosen, 1.0, 0.0).astype(bf16).reshape(rows, rows)
    parts = jnp.concatenate(split3(left[...]) + split3(right), axis=1)
    parts = nn(pick, parts).astype(bf16)
    wide = 3 * rank
    column = lax.broadcasted_iota(jnp.int32, (wide, flat), 1)
    row = lax.broadcasted_iota(jnp.int32, (wide, flat), 0) % rank
    spread = jnp.where(row == column // rank, 1.0, 0.0).astype(bf16)
    tile = jnp.where(row == column % rank, 1.0, 0.0).astype(bf16)
    over = live.astype(f32)
    step = 256
    for c in range(0, flat, step):
        product = nn(parts[:, :wide], spread[:, c : c + step]) * nn(
            parts[:, wide:], tile[:, c : c + step]
        )
        total = jnp.sum(product.reshape(seq, examples, step), axis=0)
        out[:examples, c : c + step] = total / over
    out[examples:] = queries[...]


def project(hidden_rows, output_grads, proj_in, proj_out, token_counts, queries):
    examples, seq, width = hidden_rows.shape
    model = output_grads.shape[2]
    rank = proj_in.shape[0]
    pieces = 4 if width % (4 * 128) == 0 else 1
    size = width // pieces
    anywhere = pl.BlockSpec(memory_space=pl.ANY)
    return pl.pallas_call(
        functools.partial(project_kernel, size),
        out_shape=jax.ShapeDtypeStruct((examples + queries.shape[0], rank * rank), f32),
        in_specs=[anywhere] * 4 + [
            pl.BlockSpec(memory_space=pltpu.SMEM),
            pl.BlockSpec(memory_space=pltpu.VMEM),
        ],
        out_specs=pl.BlockSpec(memory_space=pltpu.VMEM),
        scratch_shapes=[
            pltpu.VMEM((pieces, examples, seq, size), bf16),
            pltpu.VMEM(output_grads.shape, bf16),
            pltpu.VMEM((pieces, rank, size), bf16),
            pltpu.VMEM(proj_out.shape, bf16),
            pltpu.VMEM((examples * seq, rank), f32),
            pltpu.SemaphoreType.DMA((2 + 2 * pieces,)),
        ],
        compiler_params=pltpu.CompilerParams(vmem_limit_bytes=vmem_bytes),
        name="project",
    )(hidden_rows, output_grads, proj_in, proj_out, token_counts, queries)


def times(dot, x, n, passes):
    high, mid, low = split3(x)
    total = dot(high, high[:n]) + (dot(high, mid[:n]) + dot(mid, high[:n]))
    if passes > 3:
        total = total + (dot(mid, mid[:n]) + (dot(high, low[:n]) + dot(low, high[:n])))
    return total


def solve_kernel(total, each, blocks, *refs):
    bs = refs[:blocks]
    slots, out, held = refs[blocks:]
    tall, flat = bs[0].shape
    ask = tall - each
    n = each * blocks
    asked = ask * blocks

    squares = jnp.zeros((1, n), f32)
    for k in range(0, flat, n):
        x = jnp.concatenate(
            [b[:each, k : k + n] for b in bs] + [b[each:, k : k + n] for b in bs], axis=0
        )
        w = times(nt, x, n, 6)
        held[...] = w if k == 0 else held[...] + w
        squares = squares + jnp.sum(x[:n] * x[:n], axis=0, keepdims=True)
    trace = jnp.sum(squares, keepdims=True)
    gram = held[:n] * (1.0 / trace)
    scale = 2.0 * lax.rsqrt(jnp.sum(gram * gram, keepdims=True))
    held[:n] = gram * scale
    e = scale * (damp_share / flat)
    ahead = e
    for _ in range(levels):
        ahead = 2.0 * ahead * (ahead + 2.0)
    short = ahead < 1e6

    def double(passes, level, e):
        x = held[...]
        w = times(nn, x, n, passes)
        held[:n] = 4.0 * x[:n] - 2.0 * w[:n]
        held[n:] = x[n:] - w[n:] * (1.0 / (e + 2.0))
        return 2.0 * e * (e + 2.0)

    e = lax.fori_loop(0, 4, functools.partial(double, 6), e)
    more = jnp.where(jnp.sum(jnp.where(short, 1.0, 0.0)) > 0.5, 1, 0)
    e = lax.fori_loop(4, levels + more, functools.partial(double, 3), e)
    factor = (flat * total / damp_share) / trace * (e / (1.0 + e))
    mine = held[n:, :each] * factor
    place = lax.broadcasted_iota(jnp.int32, (asked, asked), 0) ^ (ask * lax.axis_index("dp"))
    pick = jnp.where(place == slots[...], 1.0, 0.0).astype(bf16)
    a, b, c = split3(mine)
    tn = (((0,), (0,)), ((), ()))
    out[...] = (
        lax.dot_general(a, pick, tn, preferred_element_type=f32)
        + lax.dot_general(b, pick, tn, preferred_element_type=f32)
        + lax.dot_general(c, pick, tn, preferred_element_type=f32)
    )


def solve(total, each, blocks, slots):
    tall, flat = blocks[0].shape
    asked = slots.shape[0]
    n = each * len(blocks)
    return pl.pallas_call(
        functools.partial(solve_kernel, total, each, len(blocks)),
        out_shape=jax.ShapeDtypeStruct((each, asked), f32),
        in_specs=[pl.BlockSpec(memory_space=pltpu.VMEM)] * (len(blocks) + 1),
        out_specs=pl.BlockSpec(memory_space=pltpu.VMEM),
        scratch_shapes=[pltpu.VMEM((n + asked, n), f32)],
        compiler_params=pltpu.CompilerParams(vmem_limit_bytes=vmem_bytes),
        name="solve",
    )(*blocks, slots.reshape(1, asked))


def flip(x, bits, size):
    return lax.ppermute(x, "dp", [(i, i ^ bits) for i in range(size)])


def gather_blocks(rows, size):
    got = {0: rows}
    for k in (8, 6, 4, 2):
        got[k] = flip(rows, k, size)
    for k in (6, 4, 2):
        got[8 + k] = flip(got[8], k, size)
    for k in (0, 8, 2, 4, 6, 10, 12, 14):
        got[k + 1] = flip(got[k], 1, size)
    return [got[k] for k in range(size)]


def dual(hidden_rows, output_grads, proj_in, proj_out, token_counts, query_vectors, query_slot):
    size = lax.axis_size("dp")
    total = hidden_rows.shape[0] * size
    rows = project(hidden_rows, output_grads, proj_in, proj_out, token_counts, query_vectors)
    blocks = gather_blocks(rows, size)
    return solve(total, hidden_rows.shape[0], blocks, query_slot)


def primal(hidden_rows, output_grads, proj_in, proj_out, token_counts, query_vectors, query_slot):
    examples, seq, width = hidden_rows.shape
    rank = proj_in.shape[0]
    flat = rank * rank
    total = examples * lax.axis_size("dp")
    left = jnp.einsum("esf,rf->esr", hidden_rows, proj_in, preferred_element_type=f32)
    right = jnp.einsum("esd,rd->esr", output_grads, proj_out, preferred_element_type=f32)
    slots = jnp.arange(seq, dtype=jnp.int32)
    masking = (slots[None, :] < token_counts[:, None]).astype(f32)
    left = left * masking[:, :, None]
    outer = jnp.einsum("esr,esq->erq", left, right, precision=lax.Precision.HIGHEST)
    vectors = (outer / token_counts.astype(f32)[:, None, None]).reshape(examples, flat)
    partial_fisher = jnp.dot(vectors.T, vectors, precision=lax.Precision.HIGHEST)
    fisher = lax.psum(partial_fisher, "dp")
    fisher = fisher / f32(total)
    trace_value = lax.psum(jnp.sum(vectors * vectors), "dp") / f32(total)
    damped = fisher + damp_share * trace_value / flat * jnp.eye(flat, dtype=f32)
    chol = jnp.linalg.cholesky(damped)
    first = lax.linalg.triangular_solve(
        chol, query_vectors, left_side=False, lower=True, transpose_a=True
    )
    solved = lax.all_gather(
        lax.linalg.triangular_solve(chol, first, left_side=False, lower=True, transpose_a=False),
        "dp",
        axis=0,
        tiled=True,
    )
    ordered = solved[query_slot]
    return jnp.dot(vectors, ordered.T, precision=lax.Precision.HIGHEST)


def shards(hidden_rows, *rest):
    size = lax.axis_size("dp")
    examples, seq, _ = hidden_rows.shape
    asked = rest[4].shape[0]
    if size == 16 and examples == 16 and seq == 16 and asked == 8:
        return dual(hidden_rows, *rest)
    return primal(hidden_rows, *rest)


def solution(mesh):
    return jax.shard_map(
        shards,
        mesh=mesh,
        in_specs=(
            P(("groups", "dp"), None, None),
            P(("groups", "dp"), None, None),
            P(),
            P(),
            P(("groups", "dp")),
            P(("groups", "dp"), None),
            P("groups"),
        ),
        out_specs=P(("groups", "dp"), None),
        check_vma=False,
    )
```

```python
import functools

import jax
import jax.numpy as jnp
from jax import lax
from jax.experimental import pallas as pl
from jax.experimental.pallas import tpu as pltpu
from jax.sharding import PartitionSpec as P

damp_share = 0.1
f32 = jnp.float32
bf16 = jnp.bfloat16
levels = 9
project_vmem = 60 * 2**20
solve_vmem = 16 * 2**20


def split3(x):
    high = x.astype(bf16)
    rest = x - high.astype(f32)
    mid = rest.astype(bf16)
    low = (rest - mid.astype(f32)).astype(bf16)
    return high, mid, low


def nt(a, b):
    return lax.dot_general(a, b, (((1,), (1,)), ((), ())), preferred_element_type=f32)


def nn(a, b):
    return jnp.dot(a, b, preferred_element_type=f32)


def project_kernel(
    size, hidden, grads, pin, pout, live_in, queries, out, hbuf, gbuf, pibuf, pobuf, left, counts, sems
):
    pieces, examples, seq, _ = hbuf.shape
    model = gbuf.shape[2]
    rank = pobuf.shape[0]
    flat = rank * rank
    rows = examples * seq
    first = [
        pltpu.make_async_copy(pout, pobuf, sems.at[0]),
        pltpu.make_async_copy(grads, gbuf, sems.at[1]),
    ]

    late = [
        pltpu.make_async_copy(live_in, counts, sems.at[2 + 2 * pieces]),
        pltpu.make_async_copy(queries, out.at[examples:], sems.at[3 + 2 * pieces]),
    ]

    def piece(i):
        across = pl.ds(pl.multiple_of(i * size, 128), size)
        return (
            pltpu.make_async_copy(pin.at[:, across], pibuf.at[i], sems.at[2 + i]),
            pltpu.make_async_copy(
                hidden.at[:, :, across], hbuf.at[i], sems.at[2 + pieces + i]
            ),
        )

    for copy in first:
        copy.start()
    for i in range(pieces):
        for copy in piece(i):
            copy.start()
    for copy in late:
        copy.start()
    for copy in first:
        copy.wait()
    left[...] = jnp.zeros((rows, rank), f32)
    right = nt(gbuf[...].reshape(rows, model), pobuf[...])

    def work(i, carry):
        for copy in piece(i):
            copy.wait()
        left[...] += nt(hbuf[i].reshape(rows, size), pibuf[i])
        return carry

    lax.fori_loop(0, pieces, work, 0)
    for copy in late:
        copy.wait()
    example = lax.broadcasted_iota(jnp.int32, (examples, 1), 0)
    live = jnp.zeros((examples, 1), jnp.int32)
    for e in range(examples):
        live = jnp.where(example == e, counts[e], live)
    to = lax.broadcasted_iota(jnp.int32, (seq, examples, rows), 1)
    slot = lax.broadcasted_iota(jnp.int32, (seq, examples, rows), 0)
    source = lax.broadcasted_iota(jnp.int32, (seq, examples, rows), 2)
    chosen = (source == to * seq + slot) & (slot < live[None])
    pick = jnp.where(chosen, 1.0, 0.0).astype(bf16).reshape(rows, rows)
    parts = jnp.concatenate(split3(left[...]) + split3(right), axis=1)
    parts = nn(pick, parts).astype(bf16)
    wide = 3 * rank
    column = lax.broadcasted_iota(jnp.int32, (wide, flat), 1)
    row = lax.broadcasted_iota(jnp.int32, (wide, flat), 0) % rank
    spread = jnp.where(row == column // rank, 1.0, 0.0).astype(bf16)
    tile = jnp.where(row == column % rank, 1.0, 0.0).astype(bf16)
    over = live.astype(f32)
    step = 256
    for c in range(0, flat, step):
        product = nn(parts[:, :wide], spread[:, c : c + step]) * nn(
            parts[:, wide:], tile[:, c : c + step]
        )
        total = jnp.sum(product.reshape(seq, examples, step), axis=0)
        out[:examples, c : c + step] = total / over


def project(hidden_rows, output_grads, proj_in, proj_out, token_counts, queries):
    examples, seq, width = hidden_rows.shape
    model = output_grads.shape[2]
    rank = proj_in.shape[0]
    pieces = 4 if width % (4 * 128) == 0 else 1
    size = width // pieces
    anywhere = pl.BlockSpec(memory_space=pl.ANY)
    return pl.pallas_call(
        functools.partial(project_kernel, size),
        out_shape=jax.ShapeDtypeStruct((examples + queries.shape[0], rank * rank), f32),
        in_specs=[anywhere] * 6,
        out_specs=pl.BlockSpec(memory_space=pltpu.VMEM),
        scratch_shapes=[
            pltpu.VMEM((pieces, examples, seq, size), bf16),
            pltpu.VMEM(output_grads.shape, bf16),
            pltpu.VMEM((pieces, rank, size), bf16),
            pltpu.VMEM(proj_out.shape, bf16),
            pltpu.VMEM((examples * seq, rank), f32),
            pltpu.SMEM(token_counts.shape, jnp.int32),
            pltpu.SemaphoreType.DMA((4 + 2 * pieces,)),
        ],
        compiler_params=pltpu.CompilerParams(vmem_limit_bytes=project_vmem),
        name="project",
    )(hidden_rows, output_grads, proj_in, proj_out, token_counts, queries)


def times(dot, x, n, passes):
    high, mid, low = split3(x)
    total = dot(high, high[:n]) + (dot(high, mid[:n]) + dot(mid, high[:n]))
    if passes > 3:
        total = total + (dot(mid, mid[:n]) + (dot(high, low[:n]) + dot(low, high[:n])))
    return total


def solve_kernel(total, each, blocks, *refs):
    bs = refs[:blocks]
    slots, out, held = refs[blocks:]
    tall, flat = bs[0].shape
    ask = tall - each
    n = each * blocks
    asked = ask * blocks

    squares = jnp.zeros((1, n), f32)
    for k in range(0, flat, n):
        x = jnp.concatenate(
            [b[:each, k : k + n] for b in bs] + [b[each:, k : k + n] for b in bs], axis=0
        )
        w = times(nt, x, n, 6)
        held[...] = w if k == 0 else held[...] + w
        squares = squares + jnp.sum(x[:n] * x[:n], axis=0, keepdims=True)
    trace = jnp.sum(squares, keepdims=True)
    gram = held[:n] * (1.0 / trace)
    scale = 2.0 * lax.rsqrt(jnp.sum(gram * gram, keepdims=True))
    held[:n] = gram * scale
    e = scale * (damp_share / flat)
    ahead = e
    for _ in range(levels):
        ahead = 2.0 * ahead * (ahead + 2.0)
    short = ahead < 1e6

    def double(passes, level, e):
        x = held[...]
        w = times(nn, x, n, passes)
        held[:n] = 4.0 * x[:n] - 2.0 * w[:n]
        held[n:] = x[n:] - w[n:] * (1.0 / (e + 2.0))
        return 2.0 * e * (e + 2.0)

    e = lax.fori_loop(0, 4, functools.partial(double, 6), e)
    more = jnp.where(jnp.sum(jnp.where(short, 1.0, 0.0)) > 0.5, 1, 0)
    e = lax.fori_loop(4, levels + more, functools.partial(double, 3), e)
    factor = (flat * total / damp_share) / trace * (e / (1.0 + e))
    mine = held[n:, :each] * factor
    place = lax.broadcasted_iota(jnp.int32, (asked, asked), 0) ^ (ask * lax.axis_index("dp"))
    pick = jnp.where(place == slots[...], 1.0, 0.0).astype(bf16)
    a, b, c = split3(mine)
    tn = (((0,), (0,)), ((), ()))
    out[...] = (
        lax.dot_general(a, pick, tn, preferred_element_type=f32)
        + lax.dot_general(b, pick, tn, preferred_element_type=f32)
        + lax.dot_general(c, pick, tn, preferred_element_type=f32)
    )


def solve(total, each, blocks, slots):
    tall, flat = blocks[0].shape
    asked = slots.shape[0]
    n = each * len(blocks)
    return pl.pallas_call(
        functools.partial(solve_kernel, total, each, len(blocks)),
        out_shape=jax.ShapeDtypeStruct((each, asked), f32),
        in_specs=[pl.BlockSpec(memory_space=pltpu.VMEM)] * (len(blocks) + 1),
        out_specs=pl.BlockSpec(memory_space=pltpu.VMEM),
        scratch_shapes=[pltpu.VMEM((n + asked, n), f32)],
        compiler_params=pltpu.CompilerParams(vmem_limit_bytes=solve_vmem),
        name="solve",
    )(*blocks, slots.reshape(1, asked))


def flip(x, bits, size):
    return lax.ppermute(x, "dp", [(i, i ^ bits) for i in range(size)])


def gather_blocks(rows, size):
    got = {0: rows}
    for k in (8, 6, 4, 2):
        got[k] = flip(rows, k, size)
    for k in (6, 4, 2):
        got[8 + k] = flip(got[8], k, size)
    for k in (0, 8, 2, 4, 6, 10, 12, 14):
        got[k + 1] = flip(got[k], 1, size)
    got[0] = flip(got[1], 1, size)
    return [got[k] for k in range(size)]


def dual(hidden_rows, output_grads, proj_in, proj_out, token_counts, query_vectors, query_slot):
    size = lax.axis_size("dp")
    total = hidden_rows.shape[0] * size
    rows = project(hidden_rows, output_grads, proj_in, proj_out, token_counts, query_vectors)
    blocks = gather_blocks(rows, size)
    return solve(total, hidden_rows.shape[0], blocks, query_slot)


def primal(hidden_rows, output_grads, proj_in, proj_out, token_counts, query_vectors, query_slot):
    examples, seq, width = hidden_rows.shape
    rank = proj_in.shape[0]
    flat = rank * rank
    total = examples * lax.axis_size("dp")
    left = jnp.einsum("esf,rf->esr", hidden_rows, proj_in, preferred_element_type=f32)
    right = jnp.einsum("esd,rd->esr", output_grads, proj_out, preferred_element_type=f32)
    slots = jnp.arange(seq, dtype=jnp.int32)
    masking = (slots[None, :] < token_counts[:, None]).astype(f32)
    left = left * masking[:, :, None]
    outer = jnp.einsum("esr,esq->erq", left, right, precision=lax.Precision.HIGHEST)
    vectors = (outer / token_counts.astype(f32)[:, None, None]).reshape(examples, flat)
    partial_fisher = jnp.dot(vectors.T, vectors, precision=lax.Precision.HIGHEST)
    fisher = lax.psum(partial_fisher, "dp")
    fisher = fisher / f32(total)
    trace_value = lax.psum(jnp.sum(vectors * vectors), "dp") / f32(total)
    damped = fisher + damp_share * trace_value / flat * jnp.eye(flat, dtype=f32)
    chol = jnp.linalg.cholesky(damped)
    first = lax.linalg.triangular_solve(
        chol, query_vectors, left_side=False, lower=True, transpose_a=True
    )
    solved = lax.all_gather(
        lax.linalg.triangular_solve(chol, first, left_side=False, lower=True, transpose_a=False),
        "dp",
        axis=0,
        tiled=True,
    )
    ordered = solved[query_slot]
    return jnp.dot(vectors, ordered.T, precision=lax.Precision.HIGHEST)


def shards(hidden_rows, *rest):
    size = lax.axis_size("dp")
    examples, seq, _ = hidden_rows.shape
    asked = rest[4].shape[0]
    if size == 16 and examples == 16 and seq == 16 and asked == 8:
        return dual(hidden_rows, *rest)
    return primal(hidden_rows, *rest)


def solution(mesh):
    return jax.shard_map(
        shards,
        mesh=mesh,
        in_specs=(
            P(("groups", "dp"), None, None),
            P(("groups", "dp"), None, None),
            P(),
            P(),
            P(("groups", "dp")),
            P(("groups", "dp"), None),
            P("groups"),
        ),
        out_specs=P(("groups", "dp"), None),
        check_vma=False,
    )
```
